512 devices in a mesh: pool: 2 (over core), dev: 64 (over y, z), rep: 4 (over x).
Axes of the slice: x: 4, y: 8, z: 8, core: 2. Of those that a mesh axis runs over, the one named last changes fastest.
Arguments:
- moe_rows: bfloat16 [4096, 4096], P(('rep', 'dev')), parts along dimension 0, may hold values from -6 to 6
- routes: int32 [4096, 8], P(('rep', 'dev')), parts along dimension 0, may hold values from 0 to 15, all different within a row; in each aligned block of 16 rows (0 to 15, 16 to 31, ...) at most 12 rows name the same one
- gate_values: float32 [4096, 8], P(('rep', 'dev')), parts along dimension 0, may hold values from 0.02 to 0.3
- gate_weight: bfloat16 [64, 4096, 256], P('dev', None, 'pool'), may hold values from -0.09375 to 0.09375
- up_weight: bfloat16 [64, 4096, 256], P('dev', None, 'pool'), may hold values from -0.09375 to 0.09375
- down_weight: bfloat16 [64, 256, 4096], P('dev', 'pool'), may hold values from -0.1875 to 0.1875
Outputs:
- expert_out: bfloat16 [4096, 4096], P(('rep', 'dev')), parts along dimension 0
The draws below stay inside these ranges and needn't reach their ends.
There are 4 independent parts, one for each index of `rep`. The reference program is written for one: setup_inputs(seed, part) draws one part's arguments, and reference() takes and returns one part's arrays. A program takes and returns all parts, laid end to end along the dimension named above; an argument that names none is the same for every part. Nothing has to cross between parts.
Inputs may be any that keep to these rules, and one draw needn't show every extreme that they name: `routes`: each row names 8 different experts. Among the rows of one device no expert is named by more than 12 rows, and in every draw some device's rows name some expert exactly 12 times.
All inputs are finite; a program needn't handle non-finite values.
Results may differ from the reference program's by a relative error of at most 0.0057.
Values may be sent and summed in bfloat16 or wider, within the bound.
No kernel may reach another device: no remote copies, remote signals or barrier semaphores. Data moves between devices by JAX's collectives and lax.ppermute only.
A program may use at most 128 MiB of HBM per device.

```python
import math
import jax
import jax.numpy as jnp
import numpy as np
from jax import lax

D = 4096
EXPERTS = 16
TOPK = 8
FF_UNITS = 1024
ROW_DEV = 16
CAP = 12
ROWS = 1024
SPLIT = 4
PIECES = 64
HID_PIECE = 256


def levels(stream_key, dims, pieces, low, top_value):
    def one(axis_at, shards_of):
        steps = jax.random.uniform(jax.random.fold_in(jax.random.fold_in(stream_key, 6), axis_at), (shards_of,), jnp.float32, low / len(pieces), top_value / len(pieces))
        return jnp.repeat(jnp.exp(steps), dims[axis_at] // shards_of).reshape((-1,) + (1,) * (len(dims) - axis_at - 1))

    factor_of = one(*pieces[0])
    for cut in pieces[1:]:
        factor_of = factor_of * one(*cut)
    return factor_of


def routed_block(key, own, number, rows, count, top, reach, skew):
    sequence = jax.random.permutation(key, count)
    crowded, common = shares(count, rows * top, reach, skew, True), shares(count, rows * top, reach, skew, False)
    places = jnp.arange(count)

    def named(lengths, offset_by):
        used = int((lengths > 0).sum())
        fixed = max(1, used // 4)
        shifted = fixed + (places - fixed + offset_by * (used - fixed)) % max(1, count - fixed)
        return jnp.zeros((count,), jnp.int32).at[sequence[jnp.where(places < fixed, places, shifted)]].set(jnp.asarray(lengths, jnp.int32))

    lengths = jnp.where(number % 4 == 0, named(crowded, number // 4), named(common, number - number // 4 - 1))
    mixed = jax.random.permutation(jax.random.fold_in(own, 3), count)
    source_of, taker = mixed[0:count // 2 * 2:2], mixed[1:count // 2 * 2:2]
    margin = jnp.minimum(lengths[source_of] - 1, reach - lengths[taker]) // 2
    margin = jnp.where((source_of == sequence[0]) | (taker == sequence[0]) | (lengths[taker] == 0), 0, jnp.maximum(margin, 0))
    shifted = jax.random.randint(jax.random.fold_in(own, 4), (count // 2,), 0, 1 << 20) % (margin + 1)
    lengths = lengths.at[source_of].add(-shifted).at[taker].add(shifted)
    items = jnp.searchsorted(jnp.cumsum(lengths), jnp.arange(rows * top), side="right").astype(jnp.int32)
    table = items.reshape(top, rows).T
    table = table[jax.random.permutation(jax.random.fold_in(own, 1), rows)]
    offset_by = jax.random.randint(jax.random.fold_in(own, 2), (rows, 1), 0, top)
    return jnp.take_along_axis(table, (jnp.arange(top)[None, :] + offset_by) % top, axis=1)


def shares(amount, total, limit, lean, full):
    weights = [(1 << 20) // math.isqrt(standing ** lean) + 1 for standing in range(1, amount + 1)]
    largest = limit if full else min(limit, max(-(-total // amount), total * weights[0] // sum(weights)))
    least = 1 if total - largest >= amount - 1 else 0
    holding, surplus = [largest] + [least] * (amount - 1), total - largest - least * (amount - 1)
    while surplus > 0:
        free = [i for i in range(1, amount) if holding[i] < largest] or [i for i in range(1, amount) if holding[i] < limit]
        pool, budget = sum([weights[i] for i in free]), surplus
        for i in free:
            extra = min(limit - holding[i], max(1, budget * weights[i] // pool), surplus)
            holding[i] = holding[i] + extra
            surplus = surplus - extra
    return np.array(holding)


def scatter_about(rng, extent, spread, most, shards=(), kind=jnp.bfloat16):
    gain = levels(rng, extent, shards, -0.22, 0.18) if shards else 1.0
    drawn = jax.random.normal(rng, extent, jnp.float32) * spread * gain
    return jnp.minimum(jnp.maximum(drawn, -most), most).astype(kind)


def setup_inputs(seed: int = 0, part: int = 0) -> dict:
    arg_keys = jax.random.split(jax.random.key(seed), 7)
    part_keys = jax.random.split(jax.random.fold_in(arg_keys[6], part), 7)
    moe_rows = scatter_about(part_keys[0], (ROWS, D), 1.0, 6.0, ((0, 64),))
    routes_keys = jax.random.split(jax.random.fold_in(part_keys[1], 1), ROWS // ROW_DEV)
    routes_turns = jax.random.permutation(jax.random.fold_in(part_keys[1], 3), ROWS // ROW_DEV)
    routes = jax.vmap(lambda own, number: routed_block(jax.random.fold_in(part_keys[1], 2), own, number, ROW_DEV, EXPERTS, TOPK, CAP, 2))(routes_keys, routes_turns).reshape((ROWS, TOPK))
    gate_values = jnp.clip(jnp.exp(math.log(0.3) - 2.7080503 * jax.random.uniform(part_keys[2], (ROWS, TOPK), jnp.float32) ** levels(part_keys[2], (ROWS, TOPK), ((0, 64),), -0.2, 0.2)), 0.02, 0.3)
    gate_weight = scatter_about(arg_keys[3], (PIECES, D, HID_PIECE), D ** -0.5, 0.09375, ((0, 64), (2, 2)))
    up_weight = scatter_about(arg_keys[4], (PIECES, D, HID_PIECE), D ** -0.5, 0.09375, ((0, 64), (2, 2)))
    down_weight = scatter_about(arg_keys[5], (PIECES, HID_PIECE, D), FF_UNITS ** -0.5, 0.1875, ((0, 64), (1, 2)))
    return dict(moe_rows=moe_rows, routes=routes, gate_values=gate_values, gate_weight=gate_weight, up_weight=up_weight, down_weight=down_weight)


def reference(moe_rows, routes, gate_values, gate_weight, up_weight, down_weight):
    expert_ids = jnp.arange(EXPERTS, dtype=jnp.int32)
    chosen = routes[:, :, None] == expert_ids[None, None, :]
    weight = jnp.sum(jnp.where(chosen, gate_values[:, :, None], 0.0), axis=1)
    gate_full = gate_weight.reshape(EXPERTS, SPLIT, D, HID_PIECE).transpose(0, 2, 1, 3).reshape(EXPERTS, D, FF_UNITS)
    up_full = up_weight.reshape(EXPERTS, SPLIT, D, HID_PIECE).transpose(0, 2, 1, 3).reshape(EXPERTS, D, FF_UNITS)
    down_full = down_weight.reshape(EXPERTS, FF_UNITS, D)
    groups = 2 * SPLIT
    group_width = FF_UNITS // groups

    def one_expert(total, inputs):
        gate_e, up_e, down_e, column = inputs
        gate_act = jnp.dot(moe_rows, gate_e, preferred_element_type=jnp.float32)
        up_act = jnp.dot(moe_rows, up_e, preferred_element_type=jnp.float32)
        act = (jax.nn.silu(gate_act) * up_act).astype(jnp.bfloat16)
        parts = jnp.einsum('rgh,ghd->rgd', act.astype(jnp.float32).reshape(ROWS, groups, group_width),
                           down_e.astype(jnp.float32).reshape(groups, group_width, D))
        parts = lax.optimization_barrier(parts.astype(jnp.bfloat16)).astype(jnp.float32)
        return total + column[:, None] * jnp.sum(parts, axis=1), None

    start_total = jnp.zeros((ROWS, D), jnp.float32)
    total, unused = lax.scan(one_expert, start_total, (gate_full, up_full, down_full, weight.T))
    return total.astype(jnp.bfloat16)
```

```python
import jax
import jax.numpy as jnp
from jax import lax
from jax.sharding import PartitionSpec as P

EXPERTS = 16
SIDE = 8
AXES = ("pool", "dev")
PAD = 128


def line_groups(side):
    along_z = [[y * side + z for z in range(side)] for y in range(side)]
    along_y = [[y * side + z for y in range(side)] for z in range(side)]
    shift = side * side
    first = along_z + [[shift + i for i in group] for group in along_y]
    second = along_y + [[shift + i for i in group] for group in along_z]
    return first, second


def body(moe_rows, routes, gate_values, gate_weight, up_weight, down_weight):
    device_count = lax.axis_size("dev")
    first, second = line_groups(SIDE)
    pool = lax.axis_index("pool")
    expert = lax.axis_index("dev") * EXPERTS // device_count
    row_count, width = moe_rows.shape
    half = row_count // 2

    expert_ids = jnp.arange(EXPERTS, dtype=jnp.int32)
    chosen = routes[:, :, None] == expert_ids[None, None, :]
    weight = jnp.sum(jnp.where(chosen, gate_values[:, :, None], 0.0), axis=1)
    high = lax.reduce_precision(weight, 8, 7)
    middle = lax.reduce_precision(weight - high, 8, 7)
    low = weight - high - middle
    terms = jnp.concatenate([high, middle, low], axis=1).astype(jnp.bfloat16)
    packed = jnp.concatenate(
        [moe_rows, jnp.pad(terms, ((0, 0), (0, PAD - 3 * EXPERTS)))], axis=1
    )
    mine = lax.dynamic_slice_in_dim(packed, pool * half, half, 0)

    swap = [(0, 1), (1, 0)]
    gate_other = lax.ppermute(gate_weight[0], "pool", swap)
    up_other = lax.ppermute(up_weight[0], "pool", swap)
    down_other = lax.ppermute(down_weight[0], "pool", swap)

    spread = jnp.broadcast_to(mine[None], (SIDE,) + mine.shape)
    line = lax.all_to_all(
        spread, AXES, split_axis=0, concat_axis=0, tiled=True, axis_index_groups=first
    ).reshape(SIDE * half, width + PAD)
    plane = lax.all_gather(line, AXES, axis=0, tiled=True, axis_index_groups=second)

    rows = plane[:, :width]
    gathered_terms = plane[:, width : width + 3 * EXPERTS].astype(jnp.float32)
    term_ids = jnp.arange(3 * EXPERTS, dtype=jnp.int32) % EXPERTS
    column = jnp.sum(jnp.where(term_ids[None, :] == expert, gathered_terms, 0.0), axis=1)

    def act_of(gate_part, up_part):
        gate_act = jnp.dot(rows, gate_part, preferred_element_type=jnp.float32)
        up_act = jnp.dot(rows, up_part, preferred_element_type=jnp.float32)
        return (jax.nn.silu(gate_act) * up_act).astype(jnp.bfloat16)

    act = jnp.concatenate(
        [act_of(gate_weight[0], up_weight[0]), act_of(gate_other, up_other)], axis=1
    )
    down = jnp.concatenate([down_weight[0], down_other], axis=0)
    part = jnp.dot(act, down, preferred_element_type=jnp.float32)
    part = (part * column[:, None]).astype(jnp.bfloat16)

    summed = lax.psum_scatter(
        part, AXES, scatter_dimension=0, tiled=True, axis_index_groups=second
    )
    returned = lax.all_to_all(
        summed.reshape(SIDE, half, width),
        AXES,
        split_axis=0,
        concat_axis=0,
        tiled=True,
        axis_index_groups=first,
    )
    total = jnp.sum(returned.astype(jnp.float32), axis=0).astype(jnp.bfloat16)
    other = lax.ppermute(total, "pool", swap)
    lower = jnp.where(pool == 0, total, other)
    upper = jnp.where(pool == 0, other, total)
    return jnp.concatenate([lower, upper], axis=0)


def solution(mesh):
    return jax.shard_map(
        body,
        mesh=mesh,
        in_specs=(
            P(("rep", "dev"), None),
            P(("rep", "dev"), None),
            P(("rep", "dev"), None),
            P("dev", None, "pool"),
            P("dev", None, "pool"),
            P("dev", "pool", None),
        ),
        out_specs=P(("rep", "dev"), None),
        check_vma=False,
    )
```

```python
import jax
import jax.numpy as jnp
from jax import lax
from jax.sharding import PartitionSpec as P

EXPERTS = 16
SIDE = 8
AXES = ("pool", "dev")
PAD = 128
REACH = SIDE // 2 - 1
SWAP = [(0, 1), (1, 0)]


def line_groups():
    along_z = [[y * SIDE + z for z in range(SIDE)] for y in range(SIDE)]
    along_y = [[y * SIDE + z for y in range(SIDE)] for z in range(SIDE)]
    shift = SIDE * SIDE
    return along_z + [[shift + i for i in group] for group in along_y]


def second_axis(other):
    places = [(y, z) for y in range(SIDE) for z in range(SIDE)]
    shift = SIDE * SIDE
    pairs = [(y * SIDE + z, other(y) * SIDE + z) for y, z in places]
    return pairs + [(shift + y * SIDE + z, shift + y * SIDE + other(z)) for y, z in places]


def neighbour_swap(odd):
    return second_axis(lambda c: (c + 1) % SIDE if c % 2 == odd else (c - 1) % SIDE)


def body(moe_rows, routes, gate_values, gate_weight, up_weight, down_weight):
    device_count = lax.axis_size("dev")
    groups = line_groups()
    odd_pairs, even_pairs = neighbour_swap(1), neighbour_swap(0)
    pool = lax.axis_index("pool")
    expert = lax.axis_index("dev") * EXPERTS // device_count
    row_count, width = moe_rows.shape
    half = row_count // 2

    expert_ids = jnp.arange(EXPERTS, dtype=jnp.int32)
    chosen = routes[:, :, None] == expert_ids[None, None, :]
    weight = jnp.sum(jnp.where(chosen, gate_values[:, :, None], 0.0), axis=1)
    high = lax.reduce_precision(weight, 8, 7)
    middle = lax.reduce_precision(weight - high, 8, 7)
    low = weight - high - middle
    terms = jnp.concatenate([high, middle, low], axis=1).astype(jnp.bfloat16)
    packed = jnp.concatenate(
        [moe_rows, jnp.pad(terms, ((0, 0), (0, PAD - 3 * EXPERTS)))], axis=1
    )
    mine = lax.dynamic_slice_in_dim(packed, pool * half, half, 0)

    cut = gate_weight.shape[2]
    spread = jnp.broadcast_to(mine[None], (SIDE,) + mine.shape)
    own = lax.all_to_all(
        spread, AXES, split_axis=0, concat_axis=0, tiled=True, axis_index_groups=groups
    ).reshape(SIDE * half, width + PAD)

    def swap_both(to_one, to_two, step):
        pairs = (odd_pairs, even_pairs) if step % 2 else (even_pairs, odd_pairs)
        return lax.ppermute(to_one, AXES, pairs[0]), lax.ppermute(to_two, AXES, pairs[1])

    one_in, two_in = [own], [own]
    for step in range(1, REACH + 1):
        from_one, from_two = swap_both(one_in[-1], two_in[-1], step)
        one_in.append(from_one)
        two_in.append(from_two)
    middle_column = width // 2
    to_one = one_in[-1][:, :middle_column]
    _, to_two = lax.optimization_barrier((to_one, two_in[-1][:, middle_column:]))
    far = jnp.concatenate(swap_both(to_one, to_two, REACH + 1), axis=1)

    gate_part, up_part, down, _ = lax.optimization_barrier(
        (gate_weight[0], up_weight[0], down_weight[0], own)
    )
    gate_up = jnp.concatenate([gate_part, up_part], axis=1)
    gate_up_other = lax.ppermute(gate_up, "pool", SWAP)
    down_other = lax.ppermute(down, "pool", SWAP)

    term_ids = jnp.arange(3 * EXPERTS, dtype=jnp.int32) % EXPERTS

    def act_of(rows, weights):
        hidden = jnp.dot(rows, weights, preferred_element_type=jnp.float32)
        return (jax.nn.silu(hidden[:, :cut]) * hidden[:, cut:]).astype(jnp.bfloat16)

    def part_of(block):
        rows = block[:, :width]
        act, act_other = act_of(rows, gate_up), act_of(rows, gate_up_other)
        column_terms = block[:, width : width + 3 * EXPERTS].astype(jnp.float32)
        column = jnp.sum(jnp.where(term_ids[None, :] == expert, column_terms, 0.0), axis=1)
        out = jnp.dot(act, down, preferred_element_type=jnp.float32)
        out = out + jnp.dot(act_other, down_other, preferred_element_type=jnp.float32)
        return out * column[:, None]

    size = SIDE * half
    far_part = part_of(far).astype(jnp.bfloat16)
    from_one, from_two = swap_both(
        far_part[:, :middle_column], far_part[:, middle_column:], REACH + 1
    )
    from_one = jnp.pad(from_one, ((0, 0), (0, width - middle_column)))
    from_two = jnp.pad(from_two, ((0, 0), (middle_column, 0)))
    for step in range(REACH, 0, -1):
        parts = part_of(jnp.concatenate([one_in[step], two_in[step]], axis=0))
        part_one, part_two = lax.optimization_barrier((parts[:size], parts[size:]))
        one_sum = part_one + from_one.astype(jnp.float32)
        two_sum = part_two + from_two.astype(jnp.float32)
        from_one, from_two = swap_both(
            one_sum.astype(jnp.bfloat16), two_sum.astype(jnp.bfloat16), step
        )
    summed = part_of(own) + from_one.astype(jnp.float32) + from_two.astype(jnp.float32)

    returned = lax.all_to_all(
        summed.astype(jnp.bfloat16).reshape(SIDE, half, width),
        AXES,
        split_axis=0,
        concat_axis=0,
        tiled=True,
        axis_index_groups=groups,
    )
    total = jnp.sum(returned.astype(jnp.float32), axis=0).astype(jnp.bfloat16)
    other = lax.ppermute(total, "pool", SWAP)
    lower = jnp.where(pool == 0, total, other)
    upper = jnp.where(pool == 0, other, total)
    return jnp.concatenate([lower, upper], axis=0)


def solution(mesh):
    return jax.shard_map(
        body,
        mesh=mesh,
        in_specs=(
            P(("rep", "dev"), None),
            P(("rep", "dev"), None),
            P(("rep", "dev"), None),
            P("dev", None, "pool"),
            P("dev", None, "pool"),
            P("dev", "pool", None),
        ),
        out_specs=P(("rep", "dev"), None),
        check_vma=False,
    )
```

```python
import jax
import jax.numpy as jnp
from jax import lax
from jax.sharding import PartitionSpec as P

EXPERTS = 16
SIDE = 8
AXES = ("pool", "dev")
PAD = 128
REACH = SIDE // 2 - 1
SWAP = [(0, 1), (1, 0)]


def line_groups():
    along_z = [[y * SIDE + z for z in range(SIDE)] for y in range(SIDE)]
    along_y = [[y * SIDE + z for y in range(SIDE)] for z in range(SIDE)]
    shift = SIDE * SIDE
    return along_z + [[shift + i for i in group] for group in along_y]


def second_axis(other):
    places = [(y, z) for y in range(SIDE) for z in range(SIDE)]
    shift = SIDE * SIDE
    pairs = [(y * SIDE + z, other(y) * SIDE + z) for y, z in places]
    return pairs + [(shift + y * SIDE + z, shift + y * SIDE + other(z)) for y, z in places]


def neighbour_swap(odd):
    return second_axis(lambda c: (c + 1) % SIDE if c % 2 == odd else (c - 1) % SIDE)


def body(moe_rows, routes, gate_values, gate_weight, up_weight, down_weight):
    device_count = lax.axis_size("dev")
    groups = line_groups()
    odd_pairs, even_pairs = neighbour_swap(1), neighbour_swap(0)
    opposite = second_axis(lambda c: (c + SIDE // 2) % SIDE)
    pool = lax.axis_index("pool")
    expert = lax.axis_index("dev") * EXPERTS // device_count
    row_count, width = moe_rows.shape
    half = row_count // 2

    expert_ids = jnp.arange(EXPERTS, dtype=jnp.int32)
    chosen = routes[:, :, None] == expert_ids[None, None, :]
    weight = jnp.sum(jnp.where(chosen, gate_values[:, :, None], 0.0), axis=1)
    high = lax.reduce_precision(weight, 8, 7)
    middle = lax.reduce_precision(weight - high, 8, 7)
    low = weight - high - middle
    terms = jnp.concatenate([high, middle, low], axis=1).astype(jnp.bfloat16)
    packed = jnp.concatenate(
        [moe_rows, jnp.pad(terms, ((0, 0), (0, PAD - 3 * EXPERTS)))], axis=1
    )
    mine = lax.dynamic_slice_in_dim(packed, pool * half, half, 0)

    cut = gate_weight.shape[2]
    spread = jnp.broadcast_to(mine[None], (SIDE,) + mine.shape)
    own = lax.all_to_all(
        spread, AXES, split_axis=0, concat_axis=0, tiled=True, axis_index_groups=groups
    ).reshape(SIDE * half, width + PAD)

    def swap_both(to_one, to_two, step):
        pairs = (odd_pairs, even_pairs) if step % 2 else (even_pairs, odd_pairs)
        return lax.ppermute(to_one, AXES, pairs[0]), lax.ppermute(to_two, AXES, pairs[1])

    one_in, two_in = [own], [own]
    far = lax.ppermute(own, AXES, opposite)
    for step in range(1, REACH + 1):
        to_one, to_two = one_in[-1], two_in[-1]
        if step == REACH:
            to_one, far = lax.optimization_barrier((to_one, far))
        from_one, from_two = swap_both(to_one, to_two, step)
        one_in.append(from_one)
        two_in.append(from_two)

    gate_part, up_part, down, _ = lax.optimization_barrier(
        (gate_weight[0], up_weight[0], down_weight[0], own)
    )
    gate_up = jnp.concatenate([gate_part, up_part], axis=1)
    gate_up_other = lax.ppermute(gate_up, "pool", SWAP)
    down_other = lax.ppermute(down, "pool", SWAP)

    term_ids = jnp.arange(3 * EXPERTS, dtype=jnp.int32) % EXPERTS

    def act_of(rows, weights):
        hidden = jnp.dot(rows, weights, preferred_element_type=jnp.float32)
        return (jax.nn.silu(hidden[:, :cut]) * hidden[:, cut:]).astype(jnp.bfloat16)

    def part_of(block):
        rows = block[:, :width]
        act, act_other = act_of(rows, gate_up), act_of(rows, gate_up_other)
        column_terms = block[:, width : width + 3 * EXPERTS].astype(jnp.float32)
        column = jnp.sum(jnp.where(term_ids[None, :] == expert, column_terms, 0.0), axis=1)
        out = jnp.dot(act, down, preferred_element_type=jnp.float32)
        out = out + jnp.dot(act_other, down_other, preferred_element_type=jnp.float32)
        return out * column[:, None]

    size = SIDE * half
    middle_column = width // 2
    far_part = part_of(far).astype(jnp.bfloat16)
    from_one, from_two = swap_both(
        far_part[:, :middle_column], far_part[:, middle_column:], REACH + 1
    )
    parts = [None]
    for step in range(1, REACH):
        parts.append(part_of(jnp.concatenate([one_in[step], two_in[step]], axis=0)))
    last_one, last_two, from_one, from_two, parts[1], parts[2] = lax.optimization_barrier(
        (one_in[REACH], two_in[REACH], from_one, from_two, parts[1], parts[2])
    )
    parts.append(part_of(jnp.concatenate([last_one, last_two], axis=0)))
    from_one = jnp.pad(from_one, ((0, 0), (0, width - middle_column)))
    from_two = jnp.pad(from_two, ((0, 0), (middle_column, 0)))
    for step in range(REACH, 0, -1):
        one_part, two_part = lax.optimization_barrier((parts[step][:size], parts[step][size:]))
        one_sum = one_part + from_one.astype(jnp.float32)
        two_sum = two_part + from_two.astype(jnp.float32)
        from_one, from_two = swap_both(
            one_sum.astype(jnp.bfloat16), two_sum.astype(jnp.bfloat16), step
        )
    summed = part_of(own) + from_one.astype(jnp.float32) + from_two.astype(jnp.float32)

    returned = lax.all_to_all(
        summed.astype(jnp.bfloat16).reshape(SIDE, half, width),
        AXES,
        split_axis=0,
        concat_axis=0,
        tiled=True,
        axis_index_groups=groups,
    )
    total = jnp.sum(returned.astype(jnp.float32), axis=0).astype(jnp.bfloat16)
    other = lax.ppermute(total, "pool", SWAP)
    lower = jnp.where(pool == 0, total, other)
    upper = jnp.where(pool == 0, other, total)
    return jnp.concatenate([lower, upper], axis=0)


def solution(mesh):
    return jax.shard_map(
        body,
        mesh=mesh,
        in_specs=(
            P(("rep", "dev"), None),
            P(("rep", "dev"), None),
            P(("rep", "dev"), None),
            P("dev", None, "pool"),
            P("dev", None, "pool"),
            P("dev", "pool", None),
        ),
        out_specs=P(("rep", "dev"), None),
        check_vma=False,
    )
```

```python
import jax
import jax.numpy as jnp
from jax import lax
from jax.sharding import PartitionSpec as P

EXPERTS = 16
SIDE = 8
AXES = ("pool", "dev")
PAD = 128
REACH = SIDE // 2 - 1
SWAP = [(0, 1), (1, 0)]


def line_groups():
    along_z = [[y * SIDE + z for z in range(SIDE)] for y in range(SIDE)]
    along_y = [[y * SIDE + z for y in range(SIDE)] for z in range(SIDE)]
    shift = SIDE * SIDE
    return along_z + [[shift + i for i in group] for group in along_y]


def second_axis(other):
    places = [(y, z) for y in range(SIDE) for z in range(SIDE)]
    shift = SIDE * SIDE
    pairs = [(y * SIDE + z, other(y) * SIDE + z) for y, z in places]
    return pairs + [(shift + y * SIDE + z, shift + y * SIDE + other(z)) for y, z in places]


def neighbour_swap(odd):
    return second_axis(lambda c: (c + 1) % SIDE if c % 2 == odd else (c - 1) % SIDE)


def body(moe_rows, routes, gate_values, gate_weight, up_weight, down_weight):
    device_count = lax.axis_size("dev")
    groups = line_groups()
    odd_pairs, even_pairs = neighbour_swap(1), neighbour_swap(0)
    opposite = second_axis(lambda c: (c + SIDE // 2) % SIDE)
    pool = lax.axis_index("pool")
    expert = lax.axis_index("dev") * EXPERTS // device_count
    row_count, width = moe_rows.shape
    half = row_count // 2

    expert_ids = jnp.arange(EXPERTS, dtype=jnp.int32)
    chosen = routes[:, :, None] == expert_ids[None, None, :]
    weight = jnp.sum(jnp.where(chosen, gate_values[:, :, None], 0.0), axis=1)
    high = lax.reduce_precision(weight, 8, 7)
    middle = lax.reduce_precision(weight - high, 8, 7)
    low = weight - high - middle
    terms = jnp.concatenate([high, middle, low], axis=1).astype(jnp.bfloat16)
    packed = jnp.concatenate(
        [moe_rows, jnp.pad(terms, ((0, 0), (0, PAD - 3 * EXPERTS)))], axis=1
    )
    mine = lax.dynamic_slice_in_dim(packed, pool * half, half, 0)

    cut = gate_weight.shape[2]
    spread = jnp.broadcast_to(mine[None], (SIDE,) + mine.shape)
    own = lax.all_to_all(
        spread, AXES, split_axis=0, concat_axis=0, tiled=True, axis_index_groups=groups
    ).reshape(SIDE * half, width + PAD)

    def swap_both(to_one, to_two, step):
        pairs = (odd_pairs, even_pairs) if step % 2 else (even_pairs, odd_pairs)
        return lax.ppermute(to_one, AXES, pairs[0]), lax.ppermute(to_two, AXES, pairs[1])

    one_in, two_in = [own], [own]
    for step in range(1, REACH + 1):
        to_one, to_two = one_in[-1], two_in[-1]
        from_one, from_two = swap_both(to_one, to_two, step)
        one_in.append(from_one)
        two_in.append(from_two)

    far = lax.ppermute(one_in[REACH], AXES, even_pairs)

    gate_part, up_part, down, _ = lax.optimization_barrier(
        (gate_weight[0], up_weight[0], down_weight[0], own)
    )
    gate_up = jnp.concatenate([gate_part, up_part], axis=1)
    gate_up_other = lax.ppermute(gate_up, "pool", SWAP)
    down_other = lax.ppermute(down, "pool", SWAP)

    term_ids = jnp.arange(3 * EXPERTS, dtype=jnp.int32) % EXPERTS

    def act_of(rows, weights):
        hidden = jnp.dot(rows, weights, preferred_element_type=jnp.float32)
        return (jax.nn.silu(hidden[:, :cut]) * hidden[:, cut:]).astype(jnp.bfloat16)

    def part_of(block):
        rows = block[:, :width]
        act, act_other = act_of(rows, gate_up), act_of(rows, gate_up_other)
        column_terms = block[:, width : width + 3 * EXPERTS].astype(jnp.float32)
        column = jnp.sum(jnp.where(term_ids[None, :] == expert, column_terms, 0.0), axis=1)
        out = jnp.dot(act, down, preferred_element_type=jnp.float32)
        out = out + jnp.dot(act_other, down_other, preferred_element_type=jnp.float32)
        return out * column[:, None]

    size = SIDE * half
    parts = [None]
    for step in range(1, REACH):
        parts.append(part_of(jnp.concatenate([one_in[step], two_in[step]], axis=0)))
    last_one, last_two, parts[1], parts[2] = lax.optimization_barrier(
        (one_in[REACH], two_in[REACH], parts[1], parts[2])
    )
    parts.append(part_of(jnp.concatenate([last_one, last_two], axis=0)))
    far_part = part_of(far).astype(jnp.bfloat16)
    from_far = lax.ppermute(far_part, AXES, opposite)
    from_one = from_two = None
    for step in range(REACH, 0, -1):
        one_sum, two_sum = lax.optimization_barrier((parts[step][:size], parts[step][size:]))
        if step < REACH:
            one_sum = one_sum + from_one.astype(jnp.float32)
            two_sum = two_sum + from_two.astype(jnp.float32)
        from_one, from_two = swap_both(
            one_sum.astype(jnp.bfloat16), two_sum.astype(jnp.bfloat16), step
        )
    own_sum = part_of(own) + from_far.astype(jnp.float32)
    summed = own_sum + from_one.astype(jnp.float32) + from_two.astype(jnp.float32)

    returned = lax.all_to_all(
        summed.astype(jnp.bfloat16).reshape(SIDE, half, width),
        AXES,
        split_axis=0,
        concat_axis=0,
        tiled=True,
        axis_index_groups=groups,
    )
    total = jnp.sum(returned.astype(jnp.float32), axis=0).astype(jnp.bfloat16)
    other = lax.ppermute(total, "pool", SWAP)
    lower = jnp.where(pool == 0, total, other)
    upper = jnp.where(pool == 0, other, total)
    return jnp.concatenate([lower, upper], axis=0)


def solution(mesh):
    return jax.shard_map(
        body,
        mesh=mesh,
        in_specs=(
            P(("rep", "dev"), None),
            P(("rep", "dev"), None),
            P(("rep", "dev"), None),
            P("dev", None, "pool"),
            P("dev", None, "pool"),
            P("dev", "pool", None),
        ),
        out_specs=P(("rep", "dev"), None),
        check_vma=False,
    )
```

```python
import jax
import jax.numpy as jnp
from jax import lax
from jax.experimental import pallas as pl
from jax.experimental.pallas import tpu as pltpu
from jax.sharding import PartitionSpec as P

EXPERTS = 16
SIDE = 8
AXES = ("pool", "dev")
PAD = 128
REACH = SIDE // 2 - 1
SWAP = [(0, 1), (1, 0)]


def line_groups():
    along_z = [[y * SIDE + z for z in range(SIDE)] for y in range(SIDE)]
    along_y = [[y * SIDE + z for y in range(SIDE)] for z in range(SIDE)]
    shift = SIDE * SIDE
    return along_z + [[shift + i for i in group] for group in along_y]


def second_axis(other):
    places = [(y, z) for y in range(SIDE) for z in range(SIDE)]
    shift = SIDE * SIDE
    pairs = [(y * SIDE + z, other(y) * SIDE + z) for y, z in places]
    return pairs + [(shift + y * SIDE + z, shift + y * SIDE + other(z)) for y, z in places]


def neighbour_swap(odd):
    return second_axis(lambda c: (c + 1) % SIDE if c % 2 == odd else (c - 1) % SIDE)


def pack_kernel(pool_ref, *refs):
    sources, out_ref, targets, done = refs[:3], refs[3], refs[4:7], refs[7]
    copies = [
        pltpu.make_async_copy(source, target, done.at[i])
        for i, (source, target) in enumerate(zip(sources, targets))
    ]
    for copy in copies:
        copy.start()
    for copy in copies:
        copy.wait()
    rows_ref, routes_ref, gates_ref = targets
    row_count, width = rows_ref.shape
    half = row_count // 2
    expert_ids = lax.broadcasted_iota(jnp.int32, (EXPERTS, row_count), 0)
    weight = jnp.zeros((EXPERTS, row_count), jnp.float32)
    for k in range(routes_ref.shape[0]):
        chosen = routes_ref[k : k + 1, :] == expert_ids
        weight = weight + jnp.where(chosen, gates_ref[k : k + 1, :], 0.0)
    high = weight.astype(jnp.bfloat16).astype(jnp.float32)
    middle = (weight - high).astype(jnp.bfloat16).astype(jnp.float32)
    low = weight - high - middle
    rest = jnp.zeros((PAD - 3 * EXPERTS, row_count), jnp.float32)
    terms = jnp.concatenate([high, middle, low, rest], axis=0).astype(jnp.bfloat16)
    across = lax.broadcasted_iota(jnp.int32, (row_count, row_count), 0)
    down = lax.broadcasted_iota(jnp.int32, (row_count, row_count), 1)
    identity = (across == down).astype(jnp.float32).astype(jnp.bfloat16)
    beside = lax.dot_general(
        identity, terms, (((1,), (1,)), ((), ())), preferred_element_type=jnp.float32
    )
    packed = jnp.concatenate([rows_ref[...].astype(jnp.float32), beside], axis=1)
    mine = jnp.where(pool_ref[0] == 0, packed[:half], packed[half:])
    out_ref[...] = jnp.concatenate([mine] * SIDE, axis=0).astype(jnp.bfloat16)


def pack(pool, moe_rows, routes, gate_values):
    row_count, width = moe_rows.shape
    hbm = pl.BlockSpec(memory_space=pltpu.HBM)
    arrays = moe_rows, routes.T, gate_values.T
    return pl.pallas_call(
        pack_kernel,
        out_shape=jax.ShapeDtypeStruct((SIDE * row_count // 2, width + PAD), jnp.bfloat16),
        in_specs=[pl.BlockSpec(memory_space=pltpu.SMEM), hbm, hbm, hbm],
        out_specs=pl.BlockSpec(memory_space=pltpu.VMEM),
        scratch_shapes=[pltpu.VMEM(a.shape, a.dtype) for a in arrays]
        + [pltpu.SemaphoreType.DMA((len(arrays),))],
        compiler_params=pltpu.CompilerParams(vmem_limit_bytes=60 * 1024 * 1024),
    )(pool.reshape(1), *arrays)


def body(moe_rows, routes, gate_values, gate_weight, up_weight, down_weight):
    device_count = lax.axis_size("dev")
    groups = line_groups()
    odd_pairs, even_pairs = neighbour_swap(1), neighbour_swap(0)
    opposite = second_axis(lambda c: (c + SIDE // 2) % SIDE)
    pool = lax.axis_index("pool")
    expert = lax.axis_index("dev") * EXPERTS // device_count
    row_count, width = moe_rows.shape
    half = row_count // 2

    cut = gate_weight.shape[2]
    spread = pack(pool, moe_rows, routes, gate_values).reshape(SIDE, half, width + PAD)
    own = lax.all_to_all(
        spread, AXES, split_axis=0, concat_axis=0, tiled=True, axis_index_groups=groups
    ).reshape(SIDE * half, width + PAD)

    def swap_both(to_one, to_two, step):
        pairs = (odd_pairs, even_pairs) if step % 2 else (even_pairs, odd_pairs)
        return lax.ppermute(to_one, AXES, pairs[0]), lax.ppermute(to_two, AXES, pairs[1])

    one_in, two_in = [own], [own]
    for step in range(1, REACH + 1):
        to_one, to_two = one_in[-1], two_in[-1]
        from_one, from_two = swap_both(to_one, to_two, step)
        one_in.append(from_one)
        two_in.append(from_two)

    far = lax.ppermute(one_in[REACH], AXES, even_pairs)

    gate_part, up_part, down, _ = lax.optimization_barrier(
        (gate_weight[0], up_weight[0], down_weight[0], own)
    )
    gate_up = jnp.concatenate([gate_part, up_part], axis=1)
    gate_up_other = lax.ppermute(gate_up, "pool", SWAP)
    down_other = lax.ppermute(down, "pool", SWAP)

    term_ids = jnp.arange(3 * EXPERTS, dtype=jnp.int32) % EXPERTS

    def act_of(rows, weights):
        hidden = jnp.dot(rows, weights, preferred_element_type=jnp.float32)
        return (jax.nn.silu(hidden[:, :cut]) * hidden[:, cut:]).astype(jnp.bfloat16)

    def part_of(block):
        rows = block[:, :width]
        act, act_other = act_of(rows, gate_up), act_of(rows, gate_up_other)
        column_terms = block[:, width : width + 3 * EXPERTS].astype(jnp.float32)
        column = jnp.sum(jnp.where(term_ids[None, :] == expert, column_terms, 0.0), axis=1)
        out = jnp.dot(act, down, preferred_element_type=jnp.float32)
        out = out + jnp.dot(act_other, down_other, preferred_element_type=jnp.float32)
        return out * column[:, None]

    size = SIDE * half
    parts = [None]
    for step in range(1, REACH):
        parts.append(part_of(jnp.concatenate([one_in[step], two_in[step]], axis=0)))
    last_one, last_two, parts[1], parts[2] = lax.optimization_barrier(
        (one_in[REACH], two_in[REACH], parts[1], parts[2])
    )
    parts.append(part_of(jnp.concatenate([last_one, last_two], axis=0)))
    far_part = part_of(far).astype(jnp.bfloat16)
    from_far = lax.ppermute(far_part, AXES, opposite)
    from_one = from_two = None
    for step in range(REACH, 0, -1):
        one_sum, two_sum = lax.optimization_barrier((parts[step][:size], parts[step][size:]))
        if step < REACH:
            one_sum = one_sum + from_one.astype(jnp.float32)
            two_sum = two_sum + from_two.astype(jnp.float32)
        from_one, from_two = swap_both(
            one_sum.astype(jnp.bfloat16), two_sum.astype(jnp.bfloat16), step
        )
    own_sum = part_of(own) + from_far.astype(jnp.float32)
    summed = own_sum + from_one.astype(jnp.float32) + from_two.astype(jnp.float32)

    returned = lax.all_to_all(
        summed.astype(jnp.bfloat16).reshape(SIDE, half, width),
        AXES,
        split_axis=0,
        concat_axis=0,
        tiled=True,
        axis_index_groups=groups,
    )
    total = jnp.sum(returned.astype(jnp.float32), axis=0).astype(jnp.bfloat16)
    other = lax.ppermute(total, "pool", SWAP)
    lower = jnp.where(pool == 0, total, other)
    upper = jnp.where(pool == 0, other, total)
    return jnp.concatenate([lower, upper], axis=0)


def solution(mesh):
    return jax.shard_map(
        body,
        mesh=mesh,
        in_specs=(
            P(("rep", "dev"), None),
            P(("rep", "dev"), None),
            P(("rep", "dev"), None),
            P("dev", None, "pool"),
            P("dev", None, "pool"),
            P("dev", "pool", None),
        ),
        out_specs=P(("rep", "dev"), None),
        check_vma=False,
    )
```

```python
import jax
import jax.numpy as jnp
from jax import lax
from jax.experimental import pallas as pl
from jax.experimental.pallas import tpu as pltpu
from jax.sharding import PartitionSpec as P

EXPERTS = 16
SIDE = 8
AXES = ("pool", "dev")
PAD = 128
REACH = SIDE // 2 - 1
SWAP = [(0, 1), (1, 0)]


def line_groups():
    along_z = [[y * SIDE + z for z in range(SIDE)] for y in range(SIDE)]
    along_y = [[y * SIDE + z for y in range(SIDE)] for z in range(SIDE)]
    shift = SIDE * SIDE
    return along_y + [[shift + i for i in group] for group in along_z]


def second_axis(other):
    places = [(y, z) for y in range(SIDE) for z in range(SIDE)]
    shift = SIDE * SIDE
    pairs = [(y * SIDE + z, y * SIDE + other(z)) for y, z in places]
    return pairs + [(shift + y * SIDE + z, shift + other(y) * SIDE + z) for y, z in places]


def neighbour_swap(odd):
    return second_axis(lambda c: (c + 1) % SIDE if c % 2 == odd else (c - 1) % SIDE)


def pack_kernel(pool_ref, *refs):
    sources, out_ref, targets, done = refs[:3], refs[3], refs[4:7], refs[7]
    copies = [
        pltpu.make_async_copy(source, target, done.at[i])
        for i, (source, target) in enumerate(zip(sources, targets))
    ]
    for copy in copies:
        copy.start()
    for copy in copies:
        copy.wait()
    rows_ref, routes_ref, gates_ref = targets
    row_count, width = rows_ref.shape
    half = row_count // 2
    expert_ids = lax.broadcasted_iota(jnp.int32, (EXPERTS, row_count), 0)
    weight = jnp.zeros((EXPERTS, row_count), jnp.float32)
    for k in range(routes_ref.shape[0]):
        chosen = routes_ref[k : k + 1, :] == expert_ids
        weight = weight + jnp.where(chosen, gates_ref[k : k + 1, :], 0.0)
    high = weight.astype(jnp.bfloat16).astype(jnp.float32)
    middle = (weight - high).astype(jnp.bfloat16).astype(jnp.float32)
    low = weight - high - middle
    rest = jnp.zeros((PAD - 3 * EXPERTS, row_count), jnp.float32)
    terms = jnp.concatenate([high, middle, low, rest], axis=0).astype(jnp.bfloat16)
    across = lax.broadcasted_iota(jnp.int32, (row_count, row_count), 0)
    down = lax.broadcasted_iota(jnp.int32, (row_count, row_count), 1)
    identity = (across == down).astype(jnp.float32).astype(jnp.bfloat16)
    beside = lax.dot_general(
        identity, terms, (((1,), (1,)), ((), ())), preferred_element_type=jnp.float32
    )
    packed = jnp.concatenate([rows_ref[...].astype(jnp.float32), beside], axis=1)
    mine = jnp.where(pool_ref[0] == 0, packed[:half], packed[half:])
    out_ref[...] = jnp.concatenate([mine] * SIDE, axis=0).astype(jnp.bfloat16)


def pack(pool, moe_rows, routes, gate_values):
    row_count, width = moe_rows.shape
    hbm = pl.BlockSpec(memory_space=pltpu.HBM)
    arrays = moe_rows, routes.T, gate_values.T
    return pl.pallas_call(
        pack_kernel,
        out_shape=jax.ShapeDtypeStruct((SIDE * row_count // 2, width + PAD), jnp.bfloat16),
        in_specs=[pl.BlockSpec(memory_space=pltpu.SMEM), hbm, hbm, hbm],
        out_specs=pl.BlockSpec(memory_space=pltpu.VMEM),
        scratch_shapes=[pltpu.VMEM(a.shape, a.dtype) for a in arrays]
        + [pltpu.SemaphoreType.DMA((len(arrays),))],
        compiler_params=pltpu.CompilerParams(vmem_limit_bytes=60 * 1024 * 1024),
    )(pool.reshape(1), *arrays)


def body(moe_rows, routes, gate_values, gate_weight, up_weight, down_weight):
    device_count = lax.axis_size("dev")
    groups = line_groups()
    odd_pairs, even_pairs = neighbour_swap(1), neighbour_swap(0)
    opposite = second_axis(lambda c: (c + SIDE // 2) % SIDE)
    pool = lax.axis_index("pool")
    expert = lax.axis_index("dev") * EXPERTS // device_count
    row_count, width = moe_rows.shape
    half = row_count // 2

    cut = gate_weight.shape[2]
    spread = pack(pool, moe_rows, routes, gate_values).reshape(SIDE, half, width + PAD)
    own = lax.all_to_all(
        spread, AXES, split_axis=0, concat_axis=0, tiled=True, axis_index_groups=groups
    ).reshape(SIDE * half, width + PAD)

    def swap_both(to_one, to_two, step):
        pairs = (odd_pairs, even_pairs) if step % 2 else (even_pairs, odd_pairs)
        return lax.ppermute(to_one, AXES, pairs[0]), lax.ppermute(to_two, AXES, pairs[1])

    one_in, two_in = [own], [own]
    for step in range(1, REACH + 1):
        to_one, to_two = one_in[-1], two_in[-1]
        from_one, from_two = swap_both(to_one, to_two, step)
        one_in.append(from_one)
        two_in.append(from_two)

    far = lax.ppermute(one_in[REACH], AXES, even_pairs)

    gate_part, up_part, down, _ = lax.optimization_barrier(
        (gate_weight[0], up_weight[0], down_weight[0], own)
    )
    gate_up = jnp.concatenate([gate_part, up_part], axis=1)
    gate_up_other = lax.ppermute(gate_up, "pool", SWAP)
    down_other = lax.ppermute(down, "pool", SWAP)

    term_ids = jnp.arange(3 * EXPERTS, dtype=jnp.int32) % EXPERTS

    def act_of(rows, weights):
        hidden = jnp.dot(rows, weights, preferred_element_type=jnp.float32)
        return (jax.nn.silu(hidden[:, :cut]) * hidden[:, cut:]).astype(jnp.bfloat16)

    def part_of(block):
        rows = block[:, :width]
        act, act_other = act_of(rows, gate_up), act_of(rows, gate_up_other)
        column_terms = block[:, width : width + 3 * EXPERTS].astype(jnp.float32)
        column = jnp.sum(jnp.where(term_ids[None, :] == expert, column_terms, 0.0), axis=1)
        out = jnp.dot(act, down, preferred_element_type=jnp.float32)
        out = out + jnp.dot(act_other, down_other, preferred_element_type=jnp.float32)
        return out * column[:, None]

    size = SIDE * half
    parts = [None]
    for step in range(1, REACH):
        parts.append(part_of(jnp.concatenate([one_in[step], two_in[step]], axis=0)))
    last_one, last_two, parts[1], parts[2] = lax.optimization_barrier(
        (one_in[REACH], two_in[REACH], parts[1], parts[2])
    )
    parts.append(part_of(jnp.concatenate([last_one, last_two], axis=0)))
    far_part = part_of(far).astype(jnp.bfloat16)
    from_far = lax.ppermute(far_part, AXES, opposite)
    from_one = from_two = None
    for step in range(REACH, 0, -1):
        one_sum, two_sum = lax.optimization_barrier((parts[step][:size], parts[step][size:]))
        if step < REACH:
            one_sum = one_sum + from_one.astype(jnp.float32)
            two_sum = two_sum + from_two.astype(jnp.float32)
        from_one, from_two = swap_both(
            one_sum.astype(jnp.bfloat16), two_sum.astype(jnp.bfloat16), step
        )
    own_sum = part_of(own) + from_far.astype(jnp.float32)
    summed = own_sum + from_one.astype(jnp.float32) + from_two.astype(jnp.float32)

    returned = lax.all_to_all(
        summed.astype(jnp.bfloat16).reshape(SIDE, half, width),
        AXES,
        split_axis=0,
        concat_axis=0,
        tiled=True,
        axis_index_groups=groups,
    )
    total = jnp.sum(returned.astype(jnp.float32), axis=0).astype(jnp.bfloat16)
    other = lax.ppermute(total, "pool", SWAP)
    lower = jnp.where(pool == 0, total, other)
    upper = jnp.where(pool == 0, other, total)
    return jnp.concatenate([lower, upper], axis=0)


def solution(mesh):
    return jax.shard_map(
        body,
        mesh=mesh,
        in_specs=(
            P(("rep", "dev"), None),
            P(("rep", "dev"), None),
            P(("rep", "dev"), None),
            P("dev", None, "pool"),
            P("dev", None, "pool"),
            P("dev", "pool", None),
        ),
        out_specs=P(("rep", "dev"), None),
        check_vma=False,
    )
```

```python
import jax
import jax.numpy as jnp
from jax import lax
from jax.experimental import pallas as pl
from jax.experimental.pallas import tpu as pltpu
from jax.sharding import PartitionSpec as P

EXPERTS = 16
SIDE = 8
AXES = ("pool", "dev")
PAD = 128
REACH = SIDE // 2 - 1
SWAP = [(0, 1), (1, 0)]


def line_groups():
    along_z = [[y * SIDE + z for z in range(SIDE)] for y in range(SIDE)]
    along_y = [[y * SIDE + z for y in range(SIDE)] for z in range(SIDE)]
    shift = SIDE * SIDE
    return along_y + [[shift + i for i in group] for group in along_z]


def second_axis(other):
    places = [(y, z) for y in range(SIDE) for z in range(SIDE)]
    shift = SIDE * SIDE
    pairs = [(y * SIDE + z, y * SIDE + other(z)) for y, z in places]
    return pairs + [(shift + y * SIDE + z, shift + other(y) * SIDE + z) for y, z in places]


def neighbour_swap(odd):
    return second_axis(lambda c: (c + 1) % SIDE if c % 2 == odd else (c - 1) % SIDE)


def pack_kernel(pool_ref, *refs):
    sources, out_ref, targets, done = refs[:3], refs[3], refs[4:7], refs[7]
    copies = [
        pltpu.make_async_copy(source, target, done.at[i])
        for i, (source, target) in enumerate(zip(sources, targets))
    ]
    for copy in copies:
        copy.start()
    for copy in copies:
        copy.wait()
    rows_ref, routes_ref, gates_ref = targets
    row_count, width = rows_ref.shape
    half = row_count // 2
    expert_ids = lax.broadcasted_iota(jnp.int32, (EXPERTS, row_count), 0)
    weight = jnp.zeros((EXPERTS, row_count), jnp.float32)
    for k in range(routes_ref.shape[0]):
        chosen = routes_ref[k : k + 1, :] == expert_ids
        weight = weight + jnp.where(chosen, gates_ref[k : k + 1, :], 0.0)
    high = weight.astype(jnp.bfloat16).astype(jnp.float32)
    middle = (weight - high).astype(jnp.bfloat16).astype(jnp.float32)
    low = weight - high - middle
    rest = jnp.zeros((PAD - 3 * EXPERTS, row_count), jnp.float32)
    terms = jnp.concatenate([high, middle, low, rest], axis=0).astype(jnp.bfloat16)
    across = lax.broadcasted_iota(jnp.int32, (row_count, row_count), 0)
    down = lax.broadcasted_iota(jnp.int32, (row_count, row_count), 1)
    identity = (across == down).astype(jnp.float32).astype(jnp.bfloat16)
    beside = lax.dot_general(
        identity, terms, (((1,), (1,)), ((), ())), preferred_element_type=jnp.float32
    )
    packed = jnp.concatenate([rows_ref[...].astype(jnp.float32), beside], axis=1)
    mine = jnp.where(pool_ref[0] == 0, packed[:half], packed[half:])
    out_ref[...] = jnp.concatenate([mine] * SIDE, axis=0).astype(jnp.bfloat16)


def pack(pool, moe_rows, routes, gate_values):
    row_count, width = moe_rows.shape
    hbm = pl.BlockSpec(memory_space=pltpu.HBM)
    arrays = moe_rows, routes.T, gate_values.T
    return pl.pallas_call(
        pack_kernel,
        out_shape=jax.ShapeDtypeStruct((SIDE * row_count // 2, width + PAD), jnp.bfloat16),
        in_specs=[pl.BlockSpec(memory_space=pltpu.SMEM), hbm, hbm, hbm],
        out_specs=pl.BlockSpec(memory_space=pltpu.VMEM),
        scratch_shapes=[pltpu.VMEM(a.shape, a.dtype) for a in arrays]
        + [pltpu.SemaphoreType.DMA((len(arrays),))],
        compiler_params=pltpu.CompilerParams(vmem_limit_bytes=60 * 1024 * 1024),
    )(pool.reshape(1), *arrays)


def body(moe_rows, routes, gate_values, gate_weight, up_weight, down_weight):
    device_count = lax.axis_size("dev")
    groups = line_groups()
    odd_pairs, even_pairs = neighbour_swap(1), neighbour_swap(0)
    opposite = second_axis(lambda c: (c + SIDE // 2) % SIDE)
    pool = lax.axis_index("pool")
    expert = lax.axis_index("dev") * EXPERTS // device_count
    row_count, width = moe_rows.shape
    half = row_count // 2

    cut = gate_weight.shape[2]
    spread = pack(pool, moe_rows, routes, gate_values).reshape(SIDE, half, width + PAD)
    own = lax.all_to_all(
        spread, AXES, split_axis=0, concat_axis=0, tiled=True, axis_index_groups=groups
    ).reshape(SIDE * half, width + PAD)

    def swap_both(to_one, to_two, step):
        pairs = (even_pairs, odd_pairs) if step % 2 else (odd_pairs, even_pairs)
        return lax.ppermute(to_one, AXES, pairs[0]), lax.ppermute(to_two, AXES, pairs[1])

    one_in, two_in = [own], [own]
    for step in range(1, REACH + 1):
        to_one, to_two = one_in[-1], two_in[-1]
        from_one, from_two = swap_both(to_one, to_two, step)
        one_in.append(from_one)
        two_in.append(from_two)

    far = lax.ppermute(one_in[REACH], AXES, odd_pairs)

    gate_part, up_part, down, _ = lax.optimization_barrier(
        (gate_weight[0], up_weight[0], down_weight[0], own)
    )
    gate_up = jnp.concatenate([gate_part, up_part], axis=1)
    gate_up_other = lax.ppermute(gate_up, "pool", SWAP)
    down_other = lax.ppermute(down, "pool", SWAP)

    term_ids = jnp.arange(3 * EXPERTS, dtype=jnp.int32) % EXPERTS

    def act_of(rows, weights):
        hidden = jnp.dot(rows, weights, preferred_element_type=jnp.float32)
        return (jax.nn.silu(hidden[:, :cut]) * hidden[:, cut:]).astype(jnp.bfloat16)

    def part_of(block):
        rows = block[:, :width]
        act, act_other = act_of(rows, gate_up), act_of(rows, gate_up_other)
        column_terms = block[:, width : width + 3 * EXPERTS].astype(jnp.float32)
        column = jnp.sum(jnp.where(term_ids[None, :] == expert, column_terms, 0.0), axis=1)
        out = jnp.dot(act, down, preferred_element_type=jnp.float32)
        out = out + jnp.dot(act_other, down_other, preferred_element_type=jnp.float32)
        return out * column[:, None]

    size = SIDE * half
    parts = [None]
    for step in range(1, REACH):
        parts.append(part_of(jnp.concatenate([one_in[step], two_in[step]], axis=0)))
    last_one, last_two, parts[1], parts[2] = lax.optimization_barrier(
        (one_in[REACH], two_in[REACH], parts[1], parts[2])
    )
    parts.append(part_of(jnp.concatenate([last_one, last_two], axis=0)))
    far_part = part_of(far).astype(jnp.bfloat16)
    from_far = lax.ppermute(far_part, AXES, opposite)
    from_one = from_two = None
    for step in range(REACH, 0, -1):
        one_sum, two_sum = lax.optimization_barrier((parts[step][:size], parts[step][size:]))
        if step < REACH:
            one_sum = one_sum + from_one.astype(jnp.float32)
            two_sum = two_sum + from_two.astype(jnp.float32)
        from_one, from_two = swap_both(
            one_sum.astype(jnp.bfloat16), two_sum.astype(jnp.bfloat16), step
        )
    own_sum = part_of(own) + from_far.astype(jnp.float32)
    summed = own_sum + from_one.astype(jnp.float32) + from_two.astype(jnp.float32)

    returned = lax.all_to_all(
        summed.astype(jnp.bfloat16).reshape(SIDE, half, width),
        AXES,
        split_axis=0,
        concat_axis=0,
        tiled=True,
        axis_index_groups=groups,
    )
    total = jnp.sum(returned.astype(jnp.float32), axis=0).astype(jnp.bfloat16)
    other = lax.ppermute(total, "pool", SWAP)
    lower = jnp.where(pool == 0, total, other)
    upper = jnp.where(pool == 0, other, total)
    return jnp.concatenate([lower, upper], axis=0)


def solution(mesh):
    return jax.shard_map(
        body,
        mesh=mesh,
        in_specs=(
            P(("rep", "dev"), None),
            P(("rep", "dev"), None),
            P(("rep", "dev"), None),
            P("dev", None, "pool"),
            P("dev", None, "pool"),
            P("dev", "pool", None),
        ),
        out_specs=P(("rep", "dev"), None),
        check_vma=False,
    )
```
